32 devices in a mesh: groups: 2 (over x), graph: 16 (over z, y, core).
Axes of the slice: x: 2, y: 2, z: 4, core: 2. Of those that a mesh axis runs over, the one named last changes fastest.
Arguments:
- var_feat: bfloat16 [65536, 256], P(('groups', 'graph')), parts along dimension 0, may hold values from -6 to 6
- con_feat: bfloat16 [32768, 256], P(('groups', 'graph')), parts along dimension 0, may hold values from -6 to 6
- tile_values: bfloat16 [2048, 128, 128], P(('groups', 'graph')), parts along dimension 0, may hold values from -0.1875 to 0.1875
- tile_row: int32 [2048], P(('groups', 'graph')), parts along dimension 0, may hold values from 0 to 7
- tile_peer: int32 [2048, 1], P(('groups', 'graph')), parts along dimension 0, may hold values from 0 to 15; in each aligned block of 64 rows (0 to 63, 64 to 127, ...) at most 4 rows name the same one
- tile_col: int32 [2048], P(('groups', 'graph')), parts along dimension 0, may hold values from 0 to 15
- labels: int32 [65536], P(('groups', 'graph')), parts along dimension 0, may hold values 0 or 1
- w_msg_var: bfloat16 [256, 256], replicated, may hold values from -0.375 to 0.375
- w_con: bfloat16 [256, 256], replicated, may hold values from -0.375 to 0.375
- w_msg_con: bfloat16 [256, 256], replicated, may hold values from -0.375 to 0.375
- w_var: bfloat16 [256, 256], replicated, may hold values from -0.375 to 0.375
- w_out: bfloat16 [256], replicated, may hold values from -0.375 to 0.375
Outputs:
- logits: float32 [65536], P(('groups', 'graph')), parts along dimension 0
- grad_msg_var: float32 [512, 256], P('groups'), parts along dimension 0
- grad_con: float32 [512, 256], P('groups'), parts along dimension 0
- grad_msg_con: float32 [512, 256], P('groups'), parts along dimension 0
- grad_var: float32 [512, 256], P('groups'), parts along dimension 0
- grad_out: float32 [512], P('groups'), parts along dimension 0
The draws below stay inside these ranges and needn't reach their ends.
There are 2 independent parts, one for each index of `groups`. The reference program is written for one: setup_inputs(seed, part) draws one part's arguments, and reference() takes and returns one part's arrays. A program takes and returns all parts, laid end to end along the dimension named above; an argument that names none is the same for every part. Nothing has to cross between parts.
Inputs may be any that keep to these rules, and one draw needn't show every extreme that they name: Among the 64 tiles held by one device, at most 4 have the same tile_peer; in every draw some device has exactly 4 tiles with one tile_peer.
All inputs are finite; a program needn't handle non-finite values. No bound on the sum of `labels` on one device may be relied on, other than what follows from the above.
Results may differ from the reference program's by a relative error of at most 0.0075.
Values may be sent and summed in bfloat16 or wider, within the bound.
A program may use at most 128 MiB of HBM per device.

```python
import math
import jax
import jax.numpy as jnp
import numpy as np
from jax import lax

D = 256
TILE_EDGE = 128
VB_DEV = 16
CB_DEV = 8
TILE_DEV = 64
CAP = 4
TILES = 1024
NVB = 256
NCB = 128
NV = 32768
NC = 16384
N_GRAPH = 16


def set_ends(result, stream_key, low, high):
    longest = result.shape.index(max(result.shape))
    spots = []
    for shift in (0, 1):
        where = [jax.random.randint(jax.random.fold_in(stream_key, axis), (), 0, length) for axis, length in enumerate(result.shape)]
        where[longest] = (where[longest] + shift) % result.shape[longest]
        spots.append(tuple(where))
    return result.at[spots[0]].set(low).at[spots[1]].set(high)


def level_of(key, extent, cuts, smallest, top_value):
    factor_of = 1.0
    for position, blocks in cuts:
        steps = jax.random.uniform(jax.random.fold_in(jax.random.fold_in(key, 6), position), (blocks,), jnp.float32, smallest / len(cuts), top_value / len(cuts))
        factor_of = factor_of * jnp.repeat(jnp.exp(steps), extent[position] // blocks).reshape((-1,) + (1,) * (len(extent) - 1 - position))
    return factor_of


def assign_block(rng, own, number, rows, amount, top, most, slope):
    ranking = jax.random.permutation(rng, amount)
    crowded, usual = load_shares(amount, rows * top, most, slope, True), load_shares(amount, rows * top, most, slope, False)
    places = jnp.arange(amount)

    def named(lengths, rotation):
        used = int((lengths > 0).sum())
        fixed = max(1, used // 4)
        moved = fixed + (places - fixed + rotation * (used - fixed)) % max(1, amount - fixed)
        return jnp.zeros((amount,), jnp.int32).at[ranking[jnp.where(places < fixed, places, moved)]].set(jnp.asarray(lengths, jnp.int32))

    lengths = jnp.where(number % 4 == 0, named(crowded, number // 4), named(usual, number - number // 4 - 1))
    mixed = jax.random.permutation(jax.random.fold_in(own, 3), amount)
    giver, receiver = mixed[0:amount // 2 * 2:2], mixed[1:amount // 2 * 2:2]
    margin = jnp.minimum(lengths[giver] - 1, most - lengths[receiver]) // 2
    margin = jnp.where((giver == ranking[0]) | (receiver == ranking[0]) | (lengths[receiver] == 0), 0, jnp.maximum(margin, 0))
    moved = jax.random.randint(jax.random.fold_in(own, 4), (amount // 2,), 0, 1 << 20) % (margin + 1)
    lengths = lengths.at[giver].add(-moved).at[receiver].add(moved)
    items = jnp.searchsorted(jnp.cumsum(lengths), jnp.arange(rows * top), side="right").astype(jnp.int32)
    grid = items.reshape(top, rows).T
    grid = grid[jax.random.permutation(jax.random.fold_in(own, 1), rows)]
    rotation = jax.random.randint(jax.random.fold_in(own, 2), (rows, 1), 0, top)
    return jnp.take_along_axis(grid, (jnp.arange(top)[None, :] + rotation) % top, axis=1)


def load_shares(count, total, most, slope, full):
    weights = [(1 << 20) // math.isqrt(rank ** slope) + 1 for rank in range(1, count + 1)]
    largest = most if full else min(most, max(-(-total // count), total * weights[0] // sum(weights)))
    least = 1 if total - largest >= count - 1 else 0
    counts, rest = [largest] + [least] * (count - 1), total - largest - least * (count - 1)
    while rest > 0:
        movable = [i for i in range(1, count) if counts[i] < largest] or [i for i in range(1, count) if counts[i] < most]
        whole, remaining = sum([weights[i] for i in movable]), rest
        for i in movable:
            more = min(most - counts[i], max(1, remaining * weights[i] // whole), rest)
            counts[i] = counts[i] + more
            rest = rest - more
    return np.array(counts)


def scatter_about(stream_key, dims, spread, bound, pieces=(), held_as=jnp.bfloat16):
    entries = spread * jax.random.normal(stream_key, dims, jnp.float32)
    if pieces:
        entries = entries * level_of(stream_key, dims, pieces, -0.22, 0.18)
    return jnp.clip(entries, -bound, bound).astype(held_as)


def setup_inputs(seed: int = 0, part: int = 0) -> dict:
    splits = jax.random.split(jax.random.key(seed), 13)
    own_keys = jax.random.split(jax.random.fold_in(splits[12], part), 13)
    var_feat = scatter_about(own_keys[0], (NV, D), 1.0, 6.0, ((0, 16),))
    con_feat = scatter_about(own_keys[1], (NC, D), 1.0, 6.0, ((0, 16),))
    tile_values = scatter_about(own_keys[2], (TILES, TILE_EDGE, TILE_EDGE), (TILE_EDGE * TILE_DEV // CB_DEV) ** -0.5, 0.1875, ((0, 16),))
    tile_row = set_ends(jax.random.randint(own_keys[3], (TILES,), 0, CB_DEV), jax.random.fold_in(own_keys[3], 1), 0, CB_DEV - 1).astype(jnp.int32)
    tile_peer_keys = jax.random.split(jax.random.fold_in(own_keys[4], 1), TILES // TILE_DEV)
    tile_peer_turns = jax.random.permutation(jax.random.fold_in(own_keys[4], 3), TILES // TILE_DEV)
    tile_peer = jax.vmap(lambda own, number: assign_block(jax.random.fold_in(own_keys[4], 2), own, number, TILE_DEV, N_GRAPH, 1, CAP, 2))(tile_peer_keys, tile_peer_turns).reshape((TILES, 1))
    tile_col = set_ends(jax.random.randint(own_keys[5], (TILES,), 0, VB_DEV), jax.random.fold_in(own_keys[5], 1), 0, VB_DEV - 1).astype(jnp.int32)
    labels = set_ends((jax.random.randint(own_keys[6], (NV,), 0, 2) < 1).astype(jnp.int32), jax.random.fold_in(own_keys[6], 1), 0, 1)
    w_msg_var = scatter_about(splits[7], (D, D), D ** -0.5, 0.375)
    w_con = scatter_about(splits[8], (D, D), D ** -0.5, 0.375)
    w_msg_con = scatter_about(splits[9], (D, D), D ** -0.5, 0.375)
    w_var = scatter_about(splits[10], (D, D), D ** -0.5, 0.375)
    w_out = scatter_about(splits[11], (D,), D ** -0.5, 0.375)
    return dict(var_feat=var_feat, con_feat=con_feat, tile_values=tile_values, tile_row=tile_row, tile_peer=tile_peer, tile_col=tile_col, labels=labels, w_msg_var=w_msg_var, w_con=w_con, w_msg_con=w_msg_con, w_var=w_var, w_out=w_out)


def silu_slope(value):
    sig = jax.nn.sigmoid(value)
    return sig * (1.0 + value * (1.0 - sig))

def reference(var_feat, con_feat, tile_values, tile_row, tile_peer, tile_col, labels, w_msg_var, w_con, w_msg_con, w_var, w_out):
    hi = lax.Precision.HIGHEST
    owner = (jnp.arange(TILES) // TILE_DEV).astype(jnp.int32)
    rows = (owner * CB_DEV + tile_row).astype(jnp.int32)
    cols = (tile_peer[:, 0] * VB_DEV + tile_col).astype(jnp.int32)
    tiles32 = tile_values.astype(jnp.float32)
    proj_var = jnp.dot(var_feat, w_msg_var, preferred_element_type=jnp.float32).astype(jnp.bfloat16)
    tile_u = proj_var.reshape(NVB, TILE_EDGE, D)[cols].astype(jnp.float32)
    messages = jnp.einsum('tij,tjd->tid', tiles32, tile_u, precision=hi)
    summed = jax.ops.segment_sum(messages, rows, NCB).reshape(NC, D)
    con_pre = summed + jnp.dot(con_feat, w_con, preferred_element_type=jnp.float32)
    con_act = jax.nn.silu(con_pre).astype(jnp.bfloat16)
    proj_con = jnp.dot(con_act, w_msg_con, preferred_element_type=jnp.float32).astype(jnp.bfloat16)
    tile_q = proj_con.reshape(NCB, TILE_EDGE, D)[rows].astype(jnp.float32)
    return_trip = jnp.einsum('tji,tjd->tid', tiles32, tile_q, precision=hi).astype(jnp.bfloat16)
    gathered = jax.ops.segment_sum(return_trip.astype(jnp.float32), cols, NVB).reshape(NV, D)
    var_pre = gathered + jnp.dot(var_feat, w_var, preferred_element_type=jnp.float32)
    var_act = jax.nn.silu(var_pre)
    out_vec = w_out.astype(jnp.float32)
    logits = jnp.dot(var_act, out_vec, precision=hi)
    scale = 1.0 / jnp.sqrt(jnp.float32(NV))
    dlog = (jax.nn.sigmoid(logits) - labels.astype(jnp.float32)) * scale
    grad_out = jnp.dot(dlog, var_act, precision=hi)
    dvar = (dlog[:, None] * out_vec[None, :] * silu_slope(var_pre)).astype(jnp.bfloat16)
    grad_var = jnp.einsum('ri,rj->ij', var_feat.astype(jnp.float32), dvar.astype(jnp.float32), precision=hi)
    tile_weight_gradient = dvar.reshape(NVB, TILE_EDGE, D)[cols].astype(jnp.float32)
    dmsg = jnp.einsum('tij,tjd->tid', tiles32, tile_weight_gradient, precision=hi)
    dproj_con = jax.ops.segment_sum(dmsg, rows, NCB).reshape(NC, D).astype(jnp.bfloat16)
    grad_msg_con = jnp.einsum('ri,rj->ij', con_act.astype(jnp.float32), dproj_con.astype(jnp.float32), precision=hi)
    dcon_pre = jnp.einsum('rj,ij->ri', dproj_con.astype(jnp.float32), w_msg_con.astype(jnp.float32), precision=hi)
    dcon = (dcon_pre * silu_slope(con_pre)).astype(jnp.bfloat16)
    grad_con = jnp.einsum('ri,rj->ij', con_feat.astype(jnp.float32), dcon.astype(jnp.float32), precision=hi)
    tile_dm = dcon.reshape(NCB, TILE_EDGE, D)[rows].astype(jnp.float32)
    tile_du = jnp.einsum('tij,tid->tjd', tiles32, tile_dm, precision=hi).astype(jnp.bfloat16)
    tile_input = var_feat.reshape(NVB, TILE_EDGE, D)[cols].astype(jnp.float32)
    grad_msg_var = jnp.einsum('tbi,tbj->ij', tile_input, tile_du.astype(jnp.float32), precision=hi)
    return (logits, grad_msg_var, grad_con, grad_msg_con, grad_var, grad_out)
```

```python
import functools

import jax
import jax.numpy as jnp
from jax import lax
from jax.experimental import pallas as pl
from jax.experimental.pallas import tpu as pltpu
from jax.sharding import PartitionSpec as P

EDGE = 128
GROUP = 4
F32 = jnp.float32
BF16 = jnp.bfloat16


def dot(a, b):
    return jnp.dot(a, b, preferred_element_type=F32)


def silu_slope(value):
    sig = jax.nn.sigmoid(value)
    return sig * (1.0 + value * (1.0 - sig))


def kernel(
    n,
    cap,
    slot_tile,
    slot_row,
    asked_of_me,
    var_feat,
    con_feat,
    tiles,
    labels,
    w_msg_var,
    w_con,
    w_msg_con,
    w_var,
    w_out,
    logits_out,
    grads_out,
    grad_out_out,
    send,
    got_feat,
    got_back,
    got_dvar,
    slot_mat,
    slot_mat_t,
    feat_t,
    con_feat_t,
    con_act_t,
    var_acc,
    con_acc,
    con_slope,
    con_half,
    dvar,
    grads,
    part_got,
    part_sum,
    total_got,
    head_part,
    head_got,
    send_sem,
    feat_sem,
    back_sem,
    dvar_sem,
    part_sem,
    total_sem,
    head_send_sem,
    head_sem,
):
    me = lax.axis_index("graph")
    lane = lax.axis_index("groups")
    blocks_v = var_feat.shape[0]
    blocks_c = con_feat.shape[0]
    scale = 1.0 / jnp.sqrt(jnp.float32(n * blocks_v * EDGE))
    turned = feat_t.shape[0] == n

    def each_peer(body):
        def step(i, carry):
            body(lax.rem(me + i, n))
            return carry

        lax.fori_loop(1, n, step, 0)

    def each_sender(body):
        def step(i, carry):
            body(lax.rem(me + n - i, n))
            return carry

        lax.fori_loop(1, n, step, 0)

    def loop(count, body):
        def step(i, carry):
            body(i)
            return carry

        lax.fori_loop(0, count, step, 0)

    def copy_to(peer, source, target, out_sem, in_sem):
        return pltpu.make_async_remote_copy(
            src_ref=source,
            dst_ref=target.at[me],
            send_sem=out_sem.at[peer],
            recv_sem=in_sem.at[me],
            device_id=(lane, peer),
            device_id_type=pl.DeviceIdType.MESH,
        )

    def copy_from(peer, source, target, out_sem, in_sem):
        return pltpu.make_async_remote_copy(
            src_ref=source,
            dst_ref=target.at[peer],
            send_sem=out_sem.at[peer],
            recv_sem=in_sem.at[peer],
            device_id=(lane, peer),
            device_id_type=pl.DeviceIdType.MESH,
        )

    barrier = pltpu.get_barrier_semaphore()

    def greet(peer):
        pl.semaphore_signal(
            barrier, inc=1, device_id=(lane, peer), device_id_type=pl.DeviceIdType.MESH
        )

    each_peer(greet)
    pl.semaphore_wait(barrier, n - 1)

    def span(c):
        return slice(c * EDGE, (c + 1) * EDGE)

    def fill(source, target, peer):
        for c in range(cap):
            index = jnp.maximum(asked_of_me[peer * cap + c], 0)
            target[peer, span(c), :] = source[index]

    def send_feat(peer):
        fill(var_feat, send, peer)
        copy_to(peer, send.at[peer], got_feat, send_sem, feat_sem).start()

    each_peer(send_feat)
    fill(var_feat, got_feat, me)

    def order_tiles(p):
        for c in range(cap):
            slot = p * cap + c
            index = slot_tile[slot]
            keep = jnp.where(index >= 0, 1.0, 0.0)
            mat = tiles[jnp.maximum(index, 0)].astype(F32) * keep
            slot_mat[slot] = mat.astype(BF16)
            slot_mat_t[slot] = mat.T.astype(BF16)

    loop(n, order_tiles)

    def self_var(b):
        var_acc[b] = dot(var_feat[b], w_var[...])

    loop(blocks_v, self_var)

    def self_con(b):
        con_acc[b] = dot(con_feat[b], w_con[...])
        con_feat_t[b] = con_feat[b].astype(F32).T.astype(BF16)

    loop(blocks_c, self_con)

    def placed(first, peer, block_of, place_of):
        rows = []
        for k in range(GROUP):
            row = []
            for c in range(cap):
                slot = peer * cap + c
                keep = jnp.where(place_of[slot] == first + k, 1.0, 0.0)
                row.append((block_of(slot) * keep).astype(BF16))
            rows.append(jnp.concatenate(row, axis=1))
        return jnp.concatenate(rows, axis=0)

    def tile_block(slot):
        return slot_mat[slot].astype(F32)

    def add_rows(acc, peer, values):
        for g in range(blocks_c // GROUP):
            part = dot(placed(g * GROUP, peer, tile_block, slot_row), values)
            acc[g * GROUP : (g + 1) * GROUP] += part.reshape(GROUP, EDGE, part.shape[1])

    def use_feat(peer):
        proj = dot(got_feat[peer], w_msg_var[...]).astype(BF16)
        add_rows(con_acc, peer, proj)

    use_feat(me)

    def take_feat(peer):
        copy_from(peer, send.at[peer], got_feat, send_sem, feat_sem).wait_recv()
        use_feat(peer)

    each_sender(take_feat)

    def activate(b):
        act = jax.nn.silu(con_acc[b])
        con_act_t[b] = act.T.astype(BF16)
        con_half[b] = dot(act.astype(BF16), w_msg_con[...]).astype(BF16)

    loop(blocks_c, activate)

    each_peer(lambda p: copy_to(p, send.at[p], got_feat, send_sem, feat_sem).wait_send())

    def back_to(peer, target):
        for c in range(cap):
            slot = peer * cap + c
            value = dot(slot_mat_t[slot], con_half[slot_row[slot]])
            target[peer, span(c), :] = value.astype(BF16)

    def send_back(peer):
        back_to(peer, send)
        copy_to(peer, send.at[peer], got_back, send_sem, back_sem).start()

    each_peer(send_back)
    back_to(me, got_back)

    def turn_feat(p):
        feat_t[p] = got_feat[p].astype(F32).T.astype(BF16)

    if turned:
        loop(n, turn_feat)

    def slope_of(b):
        con_slope[b] = silu_slope(con_acc[b])
        con_acc[b] = jnp.zeros_like(con_acc[b])

    loop(blocks_c, slope_of)

    eye = (
        lax.broadcasted_iota(jnp.int32, (EDGE, EDGE), 0)
        == lax.broadcasted_iota(jnp.int32, (EDGE, EDGE), 1)
    ).astype(F32)

    def use_back(peer):
        values = got_back[peer]

        def some(g):
            part = dot(placed(g * GROUP, peer, lambda slot: eye, asked_of_me), values)
            here = pl.ds(g * GROUP, GROUP)
            var_acc[here] = var_acc[here] + part.reshape(GROUP, EDGE, part.shape[1])

        loop(blocks_v // GROUP, some)

    use_back(me)

    def take_back(peer):
        copy_from(peer, send.at[peer], got_back, send_sem, back_sem).wait_recv()
        use_back(peer)

    each_sender(take_back)

    head = w_out[...]
    head_part[...] = jnp.zeros_like(head_part)

    def finish_var(b):
        pre = var_acc[b]
        sig = jax.nn.sigmoid(pre)
        act = pre * sig
        logit = jnp.sum(act * head, axis=1, keepdims=True)
        logits_out[b] = logit
        dlog = (jax.nn.sigmoid(logit) - labels[b].astype(F32)) * scale
        head_part[0:1, :] = head_part[0:1, :] + jnp.sum(dlog * act, axis=0, keepdims=True)
        slope = sig * (1.0 + pre * (1.0 - sig))
        dvar[b] = (dlog * head * slope).astype(BF16)

    loop(blocks_v, finish_var)

    each_peer(lambda p: copy_to(p, send.at[p], got_back, send_sem, back_sem).wait_send())

    def send_dvar(peer):
        fill(dvar, send, peer)
        copy_to(peer, send.at[peer], got_dvar, send_sem, dvar_sem).start()
        copy_to(peer, head_part, head_got, head_send_sem, head_sem).start()

    each_peer(send_dvar)
    fill(dvar, got_dvar, me)
    head_got[me] = head_part[...]

    chunk = grads.shape[1]
    width = w_con.shape[0]
    per = width // chunk

    def keep_grad(which, value):
        grads[which * per : (which + 1) * per] = value.astype(BF16).reshape(
            per, chunk, value.shape[1]
        )

    def grad_var_step(b, total):
        return total + dot(var_feat[b].astype(F32).T.astype(BF16), dvar[b])

    zero = jnp.zeros((width, w_con.shape[1]), F32)
    keep_grad(3, lax.fori_loop(0, blocks_v, grad_var_step, zero))

    add_rows(con_acc, me, got_dvar[me])

    def take_dvar(peer):
        copy_from(peer, send.at[peer], got_dvar, send_sem, dvar_sem).wait_recv()
        add_rows(con_acc, peer, got_dvar[peer])

    each_sender(take_dvar)

    grad_a = zero
    grad_b = zero
    for b in range(blocks_c):
        dproj = con_acc[b].astype(BF16)
        grad_a = grad_a + dot(con_act_t[b], dproj)
        dcon_pre = lax.dot_general(
            dproj, w_msg_con[...], (((1,), (1,)), ((), ())), preferred_element_type=F32
        )
        dcon = (dcon_pre * con_slope[b]).astype(BF16)
        con_half[b] = dcon
        grad_b = grad_b + dot(con_feat_t[b], dcon)
    keep_grad(2, grad_a)
    keep_grad(1, grad_b)

    def grad_msg_step(p, total):
        parts = []
        for c in range(cap):
            slot = p * cap + c
            parts.append(dot(slot_mat_t[slot], con_half[slot_row[slot]]).astype(BF16))
        if turned:
            left = feat_t[p]
        else:
            left = got_feat[p].astype(F32).T.astype(BF16)
        return total + dot(left, jnp.concatenate(parts, axis=0))

    keep_grad(0, lax.fori_loop(0, n, grad_msg_step, zero))

    each_peer(lambda p: copy_to(p, send.at[p], got_dvar, send_sem, dvar_sem).wait_send())
    each_peer(
        lambda p: copy_to(p, grads.at[p], part_got, send_sem, part_sem).start()
    )
    part_got[me] = grads[me]

    each_sender(
        lambda p: copy_from(p, head_part, head_got, head_send_sem, head_sem).wait()
    )
    grad_out_out[...] = jnp.sum(head_got[...], axis=0)

    each_sender(
        lambda p: copy_from(p, grads.at[p], part_got, send_sem, part_sem).wait()
    )

    def add_part(p, total):
        return total + part_got[p].astype(F32)

    total = lax.fori_loop(0, n, add_part, jnp.zeros(part_sum.shape, F32))
    part_sum[...] = total.astype(BF16)
    each_peer(lambda p: copy_to(p, part_sum, total_got, send_sem, total_sem).start())
    total_got[me] = part_sum[...]
    each_sender(
        lambda p: copy_from(p, part_sum, total_got, send_sem, total_sem).wait()
    )
    grads_out[...] = total_got[...]


def on_device(
    var_feat,
    con_feat,
    tile_values,
    tile_row,
    tile_peer,
    tile_col,
    labels,
    w_msg_var,
    w_con,
    w_msg_con,
    w_var,
    w_out,
):
    width = var_feat.shape[1]
    blocks_v = var_feat.shape[0] // EDGE
    blocks_c = con_feat.shape[0] // EDGE
    count = tile_values.shape[0]
    n = lax.axis_size("graph")
    cap = max(2, count // n)
    slots = n * cap
    peers = tile_peer[:, 0]
    order = jnp.arange(count, dtype=jnp.int32)
    earlier = (peers[:, None] == peers[None, :]) & (order[None, :] < order[:, None])
    rank = jnp.sum(earlier.astype(jnp.int32), axis=1)
    place = peers * cap + rank
    hit = place[:, None] == jnp.arange(slots, dtype=jnp.int32)[None, :]

    def by_slot(values):
        return jnp.sum(jnp.where(hit, values[:, None], 0), axis=0)

    asked = by_slot(tile_col + 1) - 1
    slot_tile = by_slot(order + 1) - 1
    slot_row = by_slot(tile_row)
    incoming = lax.all_to_all(
        asked.reshape(n, cap), "graph", split_axis=0, concat_axis=0, tiled=True
    ).reshape(slots)

    wide = cap * EDGE
    chunk = 4 * width // n
    vmem = pl.BlockSpec(memory_space=pltpu.VMEM)
    smem = pl.BlockSpec(memory_space=pltpu.SMEM)
    dma = pltpu.SemaphoreType.DMA((n,))
    logits, grads, grad_out = pl.pallas_call(
        functools.partial(kernel, n, cap),
        out_shape=(
            jax.ShapeDtypeStruct((blocks_v, EDGE, 1), F32),
            jax.ShapeDtypeStruct((n, chunk, width), BF16),
            jax.ShapeDtypeStruct((8, width), F32),
        ),
        in_specs=[smem] * 3 + [vmem] * 9,
        out_specs=(vmem, vmem, vmem),
        scratch_shapes=[
            pltpu.VMEM((n, wide, width), BF16),
            pltpu.VMEM((n, wide, width), BF16),
            pltpu.VMEM((n, wide, width), BF16),
            pltpu.VMEM((n, wide, width), BF16),
            pltpu.VMEM((slots, EDGE, EDGE), BF16),
            pltpu.VMEM((slots, EDGE, EDGE), BF16),
            pltpu.VMEM((n if slots <= count else 1, width, wide), BF16),
            pltpu.VMEM((blocks_c, width, EDGE), BF16),
            pltpu.VMEM((blocks_c, width, EDGE), BF16),
            pltpu.VMEM((blocks_v, EDGE, width), F32),
            pltpu.VMEM((blocks_c, EDGE, width), F32),
            pltpu.VMEM((blocks_c, EDGE, width), F32),
            pltpu.VMEM((blocks_c, EDGE, width), BF16),
            pltpu.VMEM((blocks_v, EDGE, width), BF16),
            pltpu.VMEM((n, chunk, width), BF16),
            pltpu.VMEM((n, chunk, width), BF16),
            pltpu.VMEM((chunk, width), BF16),
            pltpu.VMEM((n, chunk, width), BF16),
            pltpu.VMEM((8, width), F32),
            pltpu.VMEM((n, 8, width), F32),
            dma,
            dma,
            dma,
            dma,
            dma,
            dma,
            dma,
            dma,
        ],
        compiler_params=pltpu.CompilerParams(
            collective_id=0, has_side_effects=True, vmem_limit_bytes=60 * 2**20
        ),
    )(
        slot_tile,
        slot_row,
        incoming,
        var_feat.reshape(blocks_v, EDGE, width),
        con_feat.reshape(blocks_c, EDGE, width),
        tile_values,
        labels.reshape(blocks_v, EDGE, 1),
        w_msg_var,
        w_con,
        w_msg_con,
        w_var,
        w_out.astype(F32).reshape(1, width),
    )
    grads = grads.astype(F32).reshape(4, width, width)
    return (
        logits.reshape(blocks_v * EDGE),
        grads[0],
        grads[1],
        grads[2],
        grads[3],
        grad_out[0],
    )


def solution(mesh):
    rows = P(("groups", "graph"))
    whole = P("groups")
    return jax.shard_map(
        on_device,
        mesh=mesh,
        in_specs=(rows,) * 7 + (P(),) * 5,
        out_specs=(rows,) + (whole,) * 5,
        check_vma=False,
    )
```

```python
import functools

import jax
import jax.numpy as jnp
from jax import lax
from jax.experimental import pallas as pl
from jax.experimental.pallas import tpu as pltpu
from jax.sharding import PartitionSpec as P

EDGE = 128
GROUP = 4
F32 = jnp.float32
BF16 = jnp.bfloat16


def dot(a, b):
    return jnp.dot(a, b, preferred_element_type=F32)


def silu_slope(value):
    sig = jax.nn.sigmoid(value)
    return sig * (1.0 + value * (1.0 - sig))


def kernel(
    n,
    cap,
    slot_tile,
    slot_row,
    asked_of_me,
    var_feat,
    con_feat,
    tiles,
    labels,
    w_msg_var,
    w_con,
    w_msg_con,
    w_var,
    w_out,
    logits_out,
    grads_out,
    grad_out_out,
    send,
    got_feat,
    got_back,
    got_dvar,
    slot_mat,
    slot_mat_t,
    feat_t,
    con_feat_t,
    con_act_t,
    var_acc,
    con_acc,
    con_slope,
    con_half,
    dvar,
    grads,
    part_got,
    part_sum,
    total_got,
    head_part,
    head_got,
    send_sem,
    feat_sem,
    back_sem,
    dvar_sem,
    part_sem,
    total_sem,
    head_send_sem,
    head_sem,
):
    me = lax.axis_index("graph")
    lane = lax.axis_index("groups")
    blocks_v = var_feat.shape[0]
    blocks_c = con_feat.shape[0]
    scale = 1.0 / jnp.sqrt(jnp.float32(n * blocks_v * EDGE))
    turned = feat_t.shape[0] == n
    stride = 5 if n % 5 else 1

    def each_peer(body):
        def step(i, carry):
            body(lax.rem(me + stride * i, n))
            return carry

        lax.fori_loop(1, n, step, 0)

    def each_sender(body):
        def step(i, carry):
            body(lax.rem(me + stride * (n - i), n))
            return carry

        lax.fori_loop(1, n, step, 0)

    def loop(count, body):
        def step(i, carry):
            body(i)
            return carry

        lax.fori_loop(0, count, step, 0)

    def copy_to(peer, source, target, out_sem, in_sem):
        return pltpu.make_async_remote_copy(
            src_ref=source,
            dst_ref=target.at[me],
            send_sem=out_sem.at[peer],
            recv_sem=in_sem.at[me],
            device_id=(lane, peer),
            device_id_type=pl.DeviceIdType.MESH,
        )

    def copy_from(peer, source, target, out_sem, in_sem):
        return pltpu.make_async_remote_copy(
            src_ref=source,
            dst_ref=target.at[peer],
            send_sem=out_sem.at[peer],
            recv_sem=in_sem.at[peer],
            device_id=(lane, peer),
            device_id_type=pl.DeviceIdType.MESH,
        )

    barrier = pltpu.get_barrier_semaphore()

    def greet(peer):
        pl.semaphore_signal(
            barrier, inc=1, device_id=(lane, peer), device_id_type=pl.DeviceIdType.MESH
        )

    each_peer(greet)
    pl.semaphore_wait(barrier, n - 1)

    def span(c):
        return slice(c * EDGE, (c + 1) * EDGE)

    def fill(source, target, peer):
        for c in range(cap):
            index = jnp.maximum(asked_of_me[peer * cap + c], 0)
            target[peer, span(c), :] = source[index]

    def send_feat(peer):
        fill(var_feat, send, peer)
        copy_to(peer, send.at[peer], got_feat, send_sem, feat_sem).start()

    each_peer(send_feat)
    fill(var_feat, got_feat, me)

    def order_tiles(p):
        for c in range(cap):
            slot = p * cap + c
            index = slot_tile[slot]
            keep = jnp.where(index >= 0, 1.0, 0.0)
            mat = tiles[jnp.maximum(index, 0)].astype(F32) * keep
            slot_mat[slot] = mat.astype(BF16)
            slot_mat_t[slot] = mat.T.astype(BF16)

    loop(n, order_tiles)

    def self_var(b):
        var_acc[b] = dot(var_feat[b], w_var[...])

    loop(blocks_v, self_var)

    def self_con(b):
        con_acc[b] = dot(con_feat[b], w_con[...])
        con_feat_t[b] = con_feat[b].astype(F32).T.astype(BF16)

    loop(blocks_c, self_con)

    def placed(first, peer, block_of, place_of):
        rows = []
        for k in range(GROUP):
            row = []
            for c in range(cap):
                slot = peer * cap + c
                keep = jnp.where(place_of[slot] == first + k, 1.0, 0.0)
                row.append((block_of(slot) * keep).astype(BF16))
            rows.append(jnp.concatenate(row, axis=1))
        return jnp.concatenate(rows, axis=0)

    def tile_block(slot):
        return slot_mat[slot].astype(F32)

    def add_rows(acc, peer, values):
        for g in range(blocks_c // GROUP):
            part = dot(placed(g * GROUP, peer, tile_block, slot_row), values)
            acc[g * GROUP : (g + 1) * GROUP] += part.reshape(GROUP, EDGE, part.shape[1])

    def use_feat(peer):
        proj = dot(got_feat[peer], w_msg_var[...]).astype(BF16)
        add_rows(con_acc, peer, proj)

    use_feat(me)

    def take_feat(peer):
        copy_from(peer, send.at[peer], got_feat, send_sem, feat_sem).wait_recv()
        use_feat(peer)

    each_sender(take_feat)

    def activate(b):
        act = jax.nn.silu(con_acc[b])
        con_act_t[b] = act.T.astype(BF16)
        con_half[b] = dot(act.astype(BF16), w_msg_con[...]).astype(BF16)

    loop(blocks_c, activate)

    each_peer(lambda p: copy_to(p, send.at[p], got_feat, send_sem, feat_sem).wait_send())

    def back_to(peer, target):
        for c in range(cap):
            slot = peer * cap + c
            value = dot(slot_mat_t[slot], con_half[slot_row[slot]])
            target[peer, span(c), :] = value.astype(BF16)

    def send_back(peer):
        back_to(peer, send)
        copy_to(peer, send.at[peer], got_back, send_sem, back_sem).start()

    each_peer(send_back)
    back_to(me, got_back)

    def turn_feat(p):
        feat_t[p] = got_feat[p].astype(F32).T.astype(BF16)

    if turned:
        loop(n, turn_feat)

    def slope_of(b):
        con_slope[b] = silu_slope(con_acc[b])
        con_acc[b] = jnp.zeros_like(con_acc[b])

    loop(blocks_c, slope_of)

    eye = (
        lax.broadcasted_iota(jnp.int32, (EDGE, EDGE), 0)
        == lax.broadcasted_iota(jnp.int32, (EDGE, EDGE), 1)
    ).astype(F32)

    def use_back(peer):
        values = got_back[peer]

        def some(g):
            part = dot(placed(g * GROUP, peer, lambda slot: eye, asked_of_me), values)
            here = pl.ds(g * GROUP, GROUP)
            var_acc[here] = var_acc[here] + part.reshape(GROUP, EDGE, part.shape[1])

        loop(blocks_v // GROUP, some)

    use_back(me)

    def take_back(peer):
        copy_from(peer, send.at[peer], got_back, send_sem, back_sem).wait_recv()
        use_back(peer)

    each_sender(take_back)

    head = w_out[...]
    head_part[...] = jnp.zeros_like(head_part)

    def finish_var(b):
        pre = var_acc[b]
        sig = jax.nn.sigmoid(pre)
        act = pre * sig
        logit = jnp.sum(act * head, axis=1, keepdims=True)
        logits_out[b] = logit
        dlog = (jax.nn.sigmoid(logit) - labels[b].astype(F32)) * scale
        head_part[0:1, :] = head_part[0:1, :] + jnp.sum(dlog * act, axis=0, keepdims=True)
        slope = sig * (1.0 + pre * (1.0 - sig))
        dvar[b] = (dlog * head * slope).astype(BF16)

    loop(blocks_v, finish_var)

    each_peer(lambda p: copy_to(p, send.at[p], got_back, send_sem, back_sem).wait_send())

    def send_dvar(peer):
        fill(dvar, send, peer)
        copy_to(peer, send.at[peer], got_dvar, send_sem, dvar_sem).start()
        copy_to(peer, head_part, head_got, head_send_sem, head_sem).start()

    each_peer(send_dvar)
    fill(dvar, got_dvar, me)
    head_got[me] = head_part[...]

    chunk = grads.shape[1]
    width = w_con.shape[0]
    per = width // chunk

    def keep_grad(which, value):
        grads[which * per : (which + 1) * per] = value.astype(BF16).reshape(
            per, chunk, value.shape[1]
        )

    def grad_var_step(b, total):
        return total + dot(var_feat[b].astype(F32).T.astype(BF16), dvar[b])

    zero = jnp.zeros((width, w_con.shape[1]), F32)
    keep_grad(3, lax.fori_loop(0, blocks_v, grad_var_step, zero))

    add_rows(con_acc, me, got_dvar[me])

    def take_dvar(peer):
        copy_from(peer, send.at[peer], got_dvar, send_sem, dvar_sem).wait_recv()
        add_rows(con_acc, peer, got_dvar[peer])

    each_sender(take_dvar)

    grad_a = zero
    grad_b = zero
    for b in range(blocks_c):
        dproj = con_acc[b].astype(BF16)
        grad_a = grad_a + dot(con_act_t[b], dproj)
        dcon_pre = lax.dot_general(
            dproj, w_msg_con[...], (((1,), (1,)), ((), ())), preferred_element_type=F32
        )
        dcon = (dcon_pre * con_slope[b]).astype(BF16)
        con_half[b] = dcon
        grad_b = grad_b + dot(con_feat_t[b], dcon)
    keep_grad(2, grad_a)
    keep_grad(1, grad_b)

    def grad_msg_step(p, total):
        parts = []
        for c in range(cap):
            slot = p * cap + c
            parts.append(dot(slot_mat_t[slot], con_half[slot_row[slot]]).astype(BF16))
        if turned:
            left = feat_t[p]
        else:
            left = got_feat[p].astype(F32).T.astype(BF16)
        return total + dot(left, jnp.concatenate(parts, axis=0))

    keep_grad(0, lax.fori_loop(0, n, grad_msg_step, zero))

    each_peer(lambda p: copy_to(p, send.at[p], got_dvar, send_sem, dvar_sem).wait_send())
    each_peer(
        lambda p: copy_to(p, grads.at[p], part_got, send_sem, part_sem).start()
    )
    part_got[me] = grads[me]

    each_sender(
        lambda p: copy_from(p, head_part, head_got, head_send_sem, head_sem).wait()
    )
    grad_out_out[...] = jnp.sum(head_got[...], axis=0)

    each_sender(
        lambda p: copy_from(p, grads.at[p], part_got, send_sem, part_sem).wait()
    )

    def add_part(p, total):
        return total + part_got[p].astype(F32)

    total = lax.fori_loop(0, n, add_part, jnp.zeros(part_sum.shape, F32))
    part_sum[...] = total.astype(BF16)
    each_peer(lambda p: copy_to(p, part_sum, total_got, send_sem, total_sem).start())
    total_got[me] = part_sum[...]
    each_sender(
        lambda p: copy_from(p, part_sum, total_got, send_sem, total_sem).wait()
    )
    grads_out[...] = total_got[...]


def on_device(
    var_feat,
    con_feat,
    tile_values,
    tile_row,
    tile_peer,
    tile_col,
    labels,
    w_msg_var,
    w_con,
    w_msg_con,
    w_var,
    w_out,
):
    width = var_feat.shape[1]
    blocks_v = var_feat.shape[0] // EDGE
    blocks_c = con_feat.shape[0] // EDGE
    count = tile_values.shape[0]
    n = lax.axis_size("graph")
    cap = max(2, count // n)
    slots = n * cap
    peers = tile_peer[:, 0]
    order = jnp.arange(count, dtype=jnp.int32)
    earlier = (peers[:, None] == peers[None, :]) & (order[None, :] < order[:, None])
    rank = jnp.sum(earlier.astype(jnp.int32), axis=1)
    place = peers * cap + rank
    hit = place[:, None] == jnp.arange(slots, dtype=jnp.int32)[None, :]

    def by_slot(values):
        return jnp.sum(jnp.where(hit, values[:, None], 0), axis=0)

    asked = by_slot(tile_col + 1) - 1
    slot_tile = by_slot(order + 1) - 1
    slot_row = by_slot(tile_row)
    incoming = lax.all_to_all(
        asked.reshape(n, cap), "graph", split_axis=0, concat_axis=0, tiled=True
    ).reshape(slots)

    wide = cap * EDGE
    chunk = 4 * width // n
    vmem = pl.BlockSpec(memory_space=pltpu.VMEM)
    smem = pl.BlockSpec(memory_space=pltpu.SMEM)
    dma = pltpu.SemaphoreType.DMA((n,))
    logits, grads, grad_out = pl.pallas_call(
        functools.partial(kernel, n, cap),
        out_shape=(
            jax.ShapeDtypeStruct((blocks_v, EDGE, 1), F32),
            jax.ShapeDtypeStruct((n, chunk, width), BF16),
            jax.ShapeDtypeStruct((8, width), F32),
        ),
        in_specs=[smem] * 3 + [vmem] * 9,
        out_specs=(vmem, vmem, vmem),
        scratch_shapes=[
            pltpu.VMEM((n, wide, width), BF16),
            pltpu.VMEM((n, wide, width), BF16),
            pltpu.VMEM((n, wide, width), BF16),
            pltpu.VMEM((n, wide, width), BF16),
            pltpu.VMEM((slots, EDGE, EDGE), BF16),
            pltpu.VMEM((slots, EDGE, EDGE), BF16),
            pltpu.VMEM((n if slots <= count else 1, width, wide), BF16),
            pltpu.VMEM((blocks_c, width, EDGE), BF16),
            pltpu.VMEM((blocks_c, width, EDGE), BF16),
            pltpu.VMEM((blocks_v, EDGE, width), F32),
            pltpu.VMEM((blocks_c, EDGE, width), F32),
            pltpu.VMEM((blocks_c, EDGE, width), F32),
            pltpu.VMEM((blocks_c, EDGE, width), BF16),
            pltpu.VMEM((blocks_v, EDGE, width), BF16),
            pltpu.VMEM((n, chunk, width), BF16),
            pltpu.VMEM((n, chunk, width), BF16),
            pltpu.VMEM((chunk, width), BF16),
            pltpu.VMEM((n, chunk, width), BF16),
            pltpu.VMEM((8, width), F32),
            pltpu.VMEM((n, 8, width), F32),
            dma,
            dma,
            dma,
            dma,
            dma,
            dma,
            dma,
            dma,
        ],
        compiler_params=pltpu.CompilerParams(
            collective_id=0, has_side_effects=True, vmem_limit_bytes=60 * 2**20
        ),
    )(
        slot_tile,
        slot_row,
        incoming,
        var_feat.reshape(blocks_v, EDGE, width),
        con_feat.reshape(blocks_c, EDGE, width),
        tile_values,
        labels.reshape(blocks_v, EDGE, 1),
        w_msg_var,
        w_con,
        w_msg_con,
        w_var,
        w_out.astype(F32).reshape(1, width),
    )
    grads = grads.astype(F32).reshape(4, width, width)
    return (
        logits.reshape(blocks_v * EDGE),
        grads[0],
        grads[1],
        grads[2],
        grads[3],
        grad_out[0],
    )


def solution(mesh):
    rows = P(("groups", "graph"))
    whole = P("groups")
    return jax.shard_map(
        on_device,
        mesh=mesh,
        in_specs=(rows,) * 7 + (P(),) * 5,
        out_specs=(rows,) + (whole,) * 5,
        check_vma=False,
    )
```
